256 devices in a mesh: freq: 16 (over y_hi, x, core), rows: 16 (over y_lo, z).
Axes of the slice: x: 4, y: 4 (y_hi: 2, y_lo: 2; y = y_hi * 2 + y_lo), z: 8, core: 2. Of those that a mesh axis runs over, the one named last changes fastest.
Arguments:
- left_factors: bfloat16 [16, 32, 64, 2, 32, 256], P('freq', 'rows'), may hold values from -0.125 to 0.125
- right_factors: bfloat16 [16, 32, 64, 2, 32, 256], P('freq', 'rows'), may hold values from -0.25 to 0.25
- tile_ranks: int32 [16, 32, 64], P('freq', 'rows'), may hold values from 1 to 32
- window_onset: int32 [8192, 32], P('rows', 'freq'), may hold values from 1 to 33
- direct_wave: bfloat16 [16, 2, 32, 16384], P('freq', None, None, 'rows'), may hold values from -6 to 6
Outputs:
- focusing_plus: bfloat16 [16, 2, 32, 16384], P('freq', None, None, 'rows')
- focusing_minus: bfloat16 [16, 2, 32, 8192], P('freq', None, None, 'rows')
The draws below stay inside these ranges and needn't reach their ends.
Inputs may be any that keep to these rules, and one draw needn't show every extreme that they name: `tile_ranks`: the factors' columns at and beyond a tile's rank are not part of the operator. `window_onset`: the window keeps the time samples below the onset.
All inputs are finite; a program needn't handle non-finite values.
Results may differ from the reference program's by a relative error of at most 0.024.
Values may be sent and summed in bfloat16 or wider, within the bound.
No kernel may reach another device: no remote copies, remote signals or barrier semaphores. Data moves between devices by JAX's collectives and lax.ppermute only.
A program may use at most 64 MiB of HBM per device.

```python
import math
import jax
import jax.numpy as jnp
from jax import lax

TILE = 256
KMAX = 32
NR = 8192
NS = 16384
FOC = 32
ITERS = 2
NF = 16
NT = 34


def set_ends(result, rng, smallest, top_value):
    spot = [jax.random.randint(jax.random.fold_in(rng, axis), (), 0, length) for axis, length in enumerate(result.shape)]
    widest = result.shape.index(max(result.shape))
    neighbour = spot[:widest] + [(spot[widest] + 1) % result.shape[widest]] + spot[widest + 1:]
    return result.at[tuple(spot)].set(smallest).at[tuple(neighbour)].set(top_value)


def steps_of(key, dims, cuts, least, top_value):
    loudness = 1.0
    for position, blocks in cuts:
        draws = jax.random.uniform(jax.random.fold_in(jax.random.fold_in(key, 6), position), (blocks,), jnp.float32, least / len(cuts), top_value / len(cuts))
        loudness = loudness * jnp.repeat(jnp.exp(draws), dims[position] // blocks).reshape((-1,) + (1,) * (len(dims) - 1 - position))
    return loudness


def normal_values(rng, shape, deviation, limit, cuts=(), kind=jnp.bfloat16):
    array = deviation * jax.random.normal(rng, shape, jnp.float32)
    if cuts:
        array = array * steps_of(rng, shape, cuts, -0.22, 0.18)
    return jnp.clip(array, -limit, limit).astype(kind)


def setup_inputs(seed: int = 0) -> dict:
    seeds = jax.random.split(jax.random.key(seed), 6)
    left_factors = normal_values(seeds[0], (NF, NR // TILE, NS // TILE, 2, KMAX, TILE), (NS // TILE * KMAX) ** -0.5, 0.125, ((0, 16), (1, 16)))
    right_factors = normal_values(seeds[1], (NF, NR // TILE, NS // TILE, 2, KMAX, TILE), (2 * TILE) ** -0.5, 0.25, ((0, 16), (1, 16)))
    tile_ranks = set_ends(jax.random.randint(seeds[2], (NF, NR // TILE, NS // TILE), 1, KMAX + 1), jax.random.fold_in(seeds[2], 1), 1, KMAX).astype(jnp.int32)
    window_onset = set_ends(jax.random.randint(seeds[3], (NR, FOC), 1, NT), jax.random.fold_in(seeds[3], 1), 1, NT - 1).astype(jnp.int32)
    direct_wave = normal_values(seeds[4], (NF, 2, FOC, NS), 1.0, 6.0, ((0, 16), (3, 16)))
    return {"left_factors": left_factors, "right_factors": right_factors, "tile_ranks": tile_ranks, "window_onset": window_onset, "direct_wave": direct_wave}


def rank_mask(tile_ranks, width):
    levels = lax.broadcasted_iota(jnp.int32, tile_ranks.shape + (width,), tile_ranks.ndim)
    return (levels < tile_ranks[..., None]).astype(jnp.float32)

def apply_forward(left_factors, right_factors, keep_mask, gathered):
    freqs, parts, focal, sources = gathered.shape
    tile = right_factors.shape[-1]
    columns = gathered.reshape(freqs, parts, focal, sources // tile, tile).astype(jnp.float32)
    products = jnp.einsum('fijcks,fdajs->fijcdka', right_factors.astype(jnp.float32), columns, precision=lax.Precision.HIGHEST)
    real_part = products[:, :, :, 0, 0] + products[:, :, :, 1, 1]
    imag_part = products[:, :, :, 0, 1] - products[:, :, :, 1, 0]
    coefficients = (jnp.stack([real_part, imag_part], axis=3) * keep_mask[:, :, :, None, :, None]).astype(jnp.bfloat16)
    summed = jnp.einsum('fijcks,fijdka->fcdais', left_factors.astype(jnp.float32), coefficients.astype(jnp.float32), precision=lax.Precision.HIGHEST)
    real_out = summed[:, 0, 0] - summed[:, 1, 1]
    imag_out = summed[:, 0, 1] + summed[:, 1, 0]
    return jnp.stack([real_out, imag_out], axis=1).reshape(freqs, parts, focal, -1)

def apply_adjoint(left_factors, right_factors, keep_mask, minus_field):
    freqs, parts, focal, receivers = minus_field.shape
    tile = left_factors.shape[-1]
    rows_view = minus_field.reshape(freqs, parts, focal, receivers // tile, tile).astype(jnp.float32)
    products = jnp.einsum('fijcks,fdais->fijcdka', left_factors.astype(jnp.float32), rows_view, precision=lax.Precision.HIGHEST)
    real_part = products[:, :, :, 0, 0] + products[:, :, :, 1, 1]
    imag_part = products[:, :, :, 0, 1] - products[:, :, :, 1, 0]
    coefficients = (jnp.stack([real_part, imag_part], axis=3) * keep_mask[:, :, :, None, :, None]).astype(jnp.bfloat16)
    summed = jnp.einsum('fijcks,fijdka->fcdajs', right_factors.astype(jnp.float32), coefficients.astype(jnp.float32), precision=lax.Precision.HIGHEST)
    real_out = summed[:, 0, 0] - summed[:, 1, 1]
    imag_out = summed[:, 0, 1] + summed[:, 1, 0]
    return jnp.stack([real_out, imag_out], axis=1).reshape(freqs, parts, focal, -1)

def window_block(block_data, onset_part):
    count = block_data.shape[0]
    samples = 2 * count + 2
    bins = jnp.arange(count, dtype=jnp.int32) + 1
    times = jnp.arange(samples, dtype=jnp.int32)
    phase_index = bins[:, None] * times[None, :] % samples
    angle = phase_index.astype(jnp.float32) * (2.0 * math.pi / samples)
    cos_table = jnp.cos(angle)
    sin_table = jnp.sin(angle)
    norm_scale = 1.0 / math.sqrt(count + 1)
    signal = norm_scale * (jnp.einsum('kar,kt->tar', block_data[:, 0], cos_table, precision=lax.Precision.HIGHEST) - jnp.einsum('kar,kt->tar', block_data[:, 1], sin_table, precision=lax.Precision.HIGHEST))
    keep = (times[:, None, None] < jnp.transpose(onset_part)[None]).astype(jnp.float32)
    kept = signal * keep
    real_back = norm_scale * jnp.einsum('tar,kt->kar', kept, cos_table, precision=lax.Precision.HIGHEST)
    imag_back = -norm_scale * jnp.einsum('tar,kt->kar', kept, sin_table, precision=lax.Precision.HIGHEST)
    return jnp.stack([real_back, imag_back], axis=1).astype(jnp.bfloat16)

def per_frequency(function):

    def single(items):
        return function(*[item[None] for item in items])[0]
    return single

def reference(left_factors, right_factors, tile_ranks, window_onset, direct_wave):
    keep_mask = rank_mask(tile_ranks, left_factors.shape[4])
    current = direct_wave
    minus_field = None
    for iteration in range(ITERS):
        reflected = lax.map(per_frequency(apply_forward), (left_factors, right_factors, keep_mask, current))
        minus_field = window_block(reflected, window_onset)
        backward = lax.map(per_frequency(apply_adjoint), (left_factors, right_factors, keep_mask, minus_field))
        current = (direct_wave.astype(jnp.float32) + backward).astype(jnp.bfloat16)
    return (current, minus_field)
```

```python
import functools
import math

import jax
import jax.numpy as jnp
import ml_dtypes
import numpy as np
from jax import lax
from jax.experimental import pallas as pl
from jax.experimental.pallas import tpu as pltpu
from jax.sharding import PartitionSpec as P

ITERS = 2
RING = 8
HALF = RING // 2
BLOCK = 256
GROUPS = 16
SAMPLES = 34
SAMPLE_PAD = 40
F32 = jnp.float32
BF16 = jnp.bfloat16

UP = [(y * RING + z, y * RING + (z + 1) % RING) for y in range(2) for z in range(RING)]
DOWN = [(b, a) for a, b in UP]
ACROSS = [(r, (r + RING) % (2 * RING)) for r in range(2 * RING)]


def permute(value, pairs):
    return lax.ppermute(value, "rows", pairs)


def split_table(table):
    high = table.astype(ml_dtypes.bfloat16)
    low = (table - high.astype(np.float64)).astype(ml_dtypes.bfloat16)
    return np.stack([high, low])


def tables():
    bins = np.arange(GROUPS) + 1
    times = np.arange(SAMPLES)
    angle = 2.0 * math.pi * ((bins[:, None] * times[None, :]) % SAMPLES) / SAMPLES
    norm = 1.0 / math.sqrt(GROUPS + 1)
    cos_table, sin_table = norm * np.cos(angle), norm * np.sin(angle)
    to_time = np.zeros((4, 2, SAMPLE_PAD, GROUPS, 4, 2, 2))
    to_freq = np.zeros((GROUPS, 4, 2, 2, 4, 2, SAMPLE_PAD))
    for block in range(4):
        for focal in range(2):
            to_time[block, focal, :SAMPLES, :, block, 0, focal] = cos_table.T
            to_time[block, focal, :SAMPLES, :, block, 1, focal] = -sin_table.T
            to_freq[:, block, 0, focal, block, focal, :SAMPLES] = cos_table
            to_freq[:, block, 1, focal, block, focal, :SAMPLES] = -sin_table
    to_time = split_table(to_time.reshape(8 * SAMPLE_PAD, 256))
    to_freq = split_table(to_freq.reshape(256, 8 * SAMPLE_PAD))
    spread = np.zeros((4, GROUPS, 4, 2, 2, 2, GROUPS, 2))
    for block in range(4):
        for group in range(GROUPS):
            for part in range(2):
                for focal in range(2):
                    spread[block, group, block, part, focal, part, group, focal] = 1.0
    spread = spread.reshape(4, 256, 64).astype(ml_dtypes.bfloat16)
    return to_time, to_freq, spread, np.ascontiguousarray(spread.transpose(0, 2, 1))


def dot_nt(left, right):
    return lax.dot_general(left, right, (((1,), (1,)), ((), ())), preferred_element_type=F32)


def dot_nn(left, right):
    return jnp.dot(left, right, preferred_element_type=F32)


def complex_pairs(products, mask_row):
    lane = lax.broadcasted_iota(jnp.int32, products.shape, 1)
    half = products.shape[0] // 2
    turned = jnp.concatenate([products[half:], -products[:half]], axis=0)
    ahead = pltpu.roll(turned, BLOCK - 32, 1)
    behind = pltpu.roll(turned, 32, 1)
    swapped = jnp.where(lane % 64 < 32, ahead, -behind)
    return ((products + swapped) * mask_row).astype(BF16)


def column_of(lane):
    return lane // 64


def forward_kernel(count, has_start, last, _, *refs):
    chunks, rest = refs[:count], refs[count:]
    rights, rest = rest[:count], rest[count:]
    lefts, rest = rest[:count], rest[count:]
    masks, rest = rest[:count], rest[count:]
    start = None
    spread = None
    if has_start:
        start, rest = rest[0], rest[1:]
    if last:
        spread, rest = rest[0], rest[1:]
    out = rest[0]
    total = rest[1] if last else out
    step = pl.program_id(0)

    @pl.when(step == 0)
    def _():
        total[...] = start[...] if has_start else jnp.zeros_like(total)

    lane = lax.broadcasted_iota(jnp.int32, (64, BLOCK), 1)
    for n in range(count):
        stacked = jnp.concatenate([chunks[n][0, :, 256 * t : 256 * t + 256] for t in range(4)], axis=0)
        for i in range(2):
            products = dot_nt(stacked, rights[n][i])
            mine = products[0:64]
            for t in range(1, 4):
                mine = jnp.where(column_of(lane) == t, products[64 * t : 64 * t + 64], mine)
            coefficients = complex_pairs(mine, masks[n][i : i + 1, :])
            total[:, 256 * i : 256 * i + 256] += dot_nn(coefficients, lefts[n][i])

    if last:

        @pl.when(step == pl.num_programs(0) - 1)
        def _():
            rounded = total[...].astype(BF16)
            moved = dot_nn(spread[0], rounded[:, 0:128])
            for b in range(1, 4):
                moved += dot_nn(spread[b], rounded[:, 128 * b : 128 * b + 128])
            out[...] = moved.astype(BF16).reshape(GROUPS, 16, 128)


def factor_spec(n):
    return pl.BlockSpec((2, BLOCK, 256), lambda s, blocks: (0, blocks[n, s], 0))


def mask_spec(n):
    return pl.BlockSpec((2, BLOCK), lambda s, blocks: (0, blocks[n, s]))


def whole_spec(shape):
    return pl.BlockSpec(shape, lambda s, blocks: (0,) * len(shape))


CHUNK = pl.BlockSpec((1, 64, 1024), lambda s, blocks: (s, 0, 0))


def params():
    return pltpu.CompilerParams(dimension_semantics=("arbitrary",), vmem_limit_bytes=16 * 1024 * 1024)


def cost(columns):
    return pl.CostEstimate(
        flops=2 * columns * 10_000_000, bytes_accessed=columns * 150_000, transcendentals=0
    )


def forward_part(chunks, blocks, right, left, mask, start=None, spread=None):
    count, slots = len(chunks), chunks[0].shape[0]
    last = spread is not None
    operands = list(chunks) + [right] * count + [left] * count + [mask] * count
    in_specs = (
        [CHUNK] * count
        + [factor_spec(n) for n in range(count)] * 2
        + [mask_spec(n) for n in range(count)]
    )
    if start is not None:
        operands.append(start)
        in_specs.append(whole_spec((64, 512)))
    if last:
        operands.append(spread)
        in_specs.append(whole_spec((4, 256, 64)))
        out_shape = jax.ShapeDtypeStruct((GROUPS, 16, 128), BF16)
        scratch = [pltpu.VMEM((64, 512), F32)]
    else:
        out_shape = jax.ShapeDtypeStruct((64, 512), F32)
        scratch = []
    return pl.pallas_call(
        functools.partial(forward_kernel, count, start is not None, last),
        grid_spec=pltpu.PrefetchScalarGridSpec(
            num_scalar_prefetch=1,
            grid=(slots,),
            in_specs=in_specs,
            out_specs=whole_spec(out_shape.shape),
            scratch_shapes=scratch,
        ),
        out_shape=out_shape,
        compiler_params=params(),
        cost_estimate=cost(4 * count * slots),
        name="forward_part",
    )(blocks, *operands)


def adjoint_kernel(count, first, _, *refs):
    field, rest = refs[0], refs[1:]
    gather = None
    if first:
        gather, rest = rest[0], rest[1:]
    rights, rest = rest[:count], rest[count:]
    lefts, rest = rest[:count], rest[count:]
    masks, rest = rest[:count], rest[count:]
    outs, rest = rest[:count], rest[count:]
    if first:
        natural = rest[0]

        @pl.when(pl.program_id(0) == 0)
        def _():
            received = field[...].reshape(256, 128)
            for b in range(4):
                natural[:, 128 * b : 128 * b + 128] = dot_nn(gather[b], received).astype(BF16)

    else:
        natural = field
    lane = lax.broadcasted_iota(jnp.int32, (64, BLOCK), 1)
    for n in range(count):
        sums = None
        for i in range(2):
            products = dot_nt(natural[:, 256 * i : 256 * i + 256], lefts[n][i])
            coefficients = complex_pairs(products, masks[n][i : i + 1, :])
            none = jnp.zeros_like(coefficients)
            spread = jnp.concatenate(
                [jnp.where(column_of(lane) == t, coefficients, none) for t in range(4)], axis=0
            )
            part = dot_nn(spread, rights[n][i])
            sums = part if sums is None else sums + part
        sums = sums.astype(BF16)
        for t in range(4):
            outs[n][0, :, 256 * t : 256 * t + 256] = sums[64 * t : 64 * t + 64]


def adjoint_part(field, blocks, right, left, mask, gather=None):
    count, slots = blocks.shape
    first = gather is not None
    operands, in_specs = [field], [whole_spec(field.shape)]
    if first:
        operands.append(gather)
        in_specs.append(whole_spec((4, 64, 256)))
    operands += [right] * count + [left] * count + [mask] * count
    in_specs += [factor_spec(n) for n in range(count)] * 2 + [mask_spec(n) for n in range(count)]
    out_shape = [jax.ShapeDtypeStruct((slots, 64, 1024), BF16)] * count
    out_specs = [CHUNK] * count
    if first:
        out_shape.append(jax.ShapeDtypeStruct((64, 512), BF16))
        out_specs.append(whole_spec((64, 512)))
    return pl.pallas_call(
        functools.partial(adjoint_kernel, count, first),
        grid_spec=pltpu.PrefetchScalarGridSpec(
            num_scalar_prefetch=1, grid=(slots,), in_specs=in_specs, out_specs=out_specs
        ),
        out_shape=out_shape,
        compiler_params=params(),
        cost_estimate=cost(4 * count * slots),
        name="adjoint_part",
    )(blocks, *operands)


def window_kernel(field, onset, to_time, to_freq, out):
    received = field[...].reshape(256, 128)
    signal = dot_nn(to_time[0], received) + dot_nn(to_time[1], received)
    signal = signal.reshape(8, SAMPLE_PAD, 128)
    time = lax.broadcasted_iota(jnp.int32, signal.shape, 1)
    kept = jnp.where(time < onset[...][:, None, :], signal, 0.0).reshape(8 * SAMPLE_PAD, 128)
    high = kept.astype(BF16)
    low = (kept - high.astype(F32)).astype(BF16)
    back = dot_nn(to_freq[0], high) + dot_nn(to_freq[1], high) + dot_nn(to_freq[0], low)
    out[...] = back.astype(BF16).reshape(GROUPS, 16, 128)


def window_block(field, onset, to_time, to_freq):
    return pl.pallas_call(
        window_kernel,
        out_shape=jax.ShapeDtypeStruct((GROUPS, 16, 128), BF16),
        compiler_params=pltpu.CompilerParams(vmem_limit_bytes=16 * 1024 * 1024),
        cost_estimate=pl.CostEstimate(flops=200_000_000, bytes_accessed=1_000_000, transcendentals=0),
        name="window",
    )(field, onset, to_time, to_freq)


def exchange(value):
    return lax.all_to_all(value, "freq", split_axis=0, concat_axis=0, tiled=True)


def add(*terms):
    total = terms[0].astype(F32)
    for term in terms[1:]:
        total = total + term.astype(F32)
    return total.astype(BF16)


def on_device(left_factors, right_factors, tile_ranks, window_onset, direct_wave):
    left = left_factors.reshape(2, 4096, 256)
    right = right_factors.reshape(2, 4096, 256)
    levels = lax.broadcasted_iota(jnp.int32, (2, 64, 2, 32), 3)
    mask = (levels < tile_ranks.reshape(2, 64, 1, 1)).astype(F32).reshape(2, 4096)
    onset = jnp.transpose(window_onset.reshape(4, 128, 2), (0, 2, 1)).reshape(8, 128)
    to_time, to_freq, spread, gather = [jnp.asarray(table) for table in tables()]

    place = lax.axis_index("rows")
    row, spot = place // RING, place % RING

    def blocks_of(*shifts):
        own = [row * RING, (1 - row) * RING]
        return jnp.stack(
            [jnp.stack([base + (spot + shift) % RING for base in own]) for shift in shifts]
        ).astype(jnp.int32)

    ring_blocks = {step: blocks_of(-step, step) for step in range(1, HALF)}
    own_blocks = blocks_of(0)
    far_blocks = blocks_of(HALF)

    direct = direct_wave.reshape(64, 1024)
    direct_pair = jnp.stack([direct, permute(direct, ACROSS)])
    pair = direct_pair
    minus_field = None
    current = None
    for iteration in range(ITERS):
        up = down = pair
        total = forward_part([pair], own_blocks, right, left, mask)
        for step in range(1, HALF):
            up, down = permute(up, UP), permute(down, DOWN)
            total = forward_part([up, down], ring_blocks[step], right, left, mask, start=total)
        far = [permute(up[0:1], UP), permute(down[1:2], DOWN)]
        reflected = forward_part(
            far, far_blocks.reshape(2, 1), right, left, mask, start=total, spread=spread
        )
        windowed = window_block(exchange(reflected), onset, to_time, to_freq)
        received = exchange(windowed)
        far_first, far_second, minus_field = adjoint_part(
            received, far_blocks.reshape(2, 1), right, left, mask, gather=gather
        )
        up, down = permute(far_first, UP), permute(far_second, DOWN)
        for step in range(HALF - 1, 0, -1):
            to_up, to_down = adjoint_part(minus_field, blocks_of(step, -step), right, left, mask)
            if step == HALF - 1:
                to_up = jnp.concatenate([add(to_up[0:1], up), to_up[1:2]], axis=0)
                to_down = jnp.concatenate([to_down[0:1], add(to_down[1:2], down)], axis=0)
            else:
                to_up, to_down = add(to_up, up), add(to_down, down)
            up, down = permute(to_up, UP), permute(to_down, DOWN)
        (own,) = adjoint_part(minus_field, own_blocks, right, left, mask)
        if iteration < ITERS - 1:
            summed = add(own, up, down)
            other = permute(summed, ACROSS)
            pair = add(direct_pair, summed, other[::-1])
        else:
            other = permute(add(own[1], up[1], down[1]), ACROSS)
            current = add(direct, own[0], up[0], down[0], other)
    return (current.reshape(1, 2, 32, 1024), minus_field.reshape(1, 2, 32, 512))


def solution(mesh):
    in_specs = (
        P("freq", "rows", None, None, None, None),
        P("freq", "rows", None, None, None, None),
        P("freq", "rows", None),
        P("rows", "freq"),
        P("freq", None, None, "rows"),
    )
    out_specs = (P("freq", None, None, "rows"), P("freq", None, None, "rows"))
    return jax.shard_map(
        on_device, mesh=mesh, in_specs=in_specs, out_specs=out_specs, check_vma=False
    )
```

```python
import functools
import math

import jax
import jax.numpy as jnp
import ml_dtypes
import numpy as np
from jax import lax
from jax.experimental import pallas as pl
from jax.experimental.pallas import tpu as pltpu
from jax.sharding import PartitionSpec as P

ITERS = 2
RING = 8
HALF = RING // 2
BLOCK = 256
GROUPS = 16
SAMPLES = 34
SAMPLE_PAD = 40
F32 = jnp.float32
BF16 = jnp.bfloat16

UP = [(y * RING + z, y * RING + (z + 1) % RING) for y in range(2) for z in range(RING)]
DOWN = [(b, a) for a, b in UP]
ACROSS = [(r, (r + RING) % (2 * RING)) for r in range(2 * RING)]


def permute(value, pairs):
    return lax.ppermute(value, "rows", pairs)


def split_table(table):
    high = table.astype(ml_dtypes.bfloat16)
    low = (table - high.astype(np.float64)).astype(ml_dtypes.bfloat16)
    return np.stack([high, low])


def tables():
    bins = np.arange(GROUPS) + 1
    times = np.arange(SAMPLES)
    angle = 2.0 * math.pi * ((bins[:, None] * times[None, :]) % SAMPLES) / SAMPLES
    norm = 1.0 / math.sqrt(GROUPS + 1)
    cos_table, sin_table = norm * np.cos(angle), norm * np.sin(angle)
    to_time = np.zeros((4, 2, SAMPLE_PAD, GROUPS, 4, 2, 2))
    to_freq = np.zeros((GROUPS, 4, 2, 2, 4, 2, SAMPLE_PAD))
    for block in range(4):
        for focal in range(2):
            to_time[block, focal, :SAMPLES, :, block, 0, focal] = cos_table.T
            to_time[block, focal, :SAMPLES, :, block, 1, focal] = -sin_table.T
            to_freq[:, block, 0, focal, block, focal, :SAMPLES] = cos_table
            to_freq[:, block, 1, focal, block, focal, :SAMPLES] = -sin_table
    to_time = split_table(to_time.reshape(8 * SAMPLE_PAD, 256))
    to_freq = split_table(to_freq.reshape(256, 8 * SAMPLE_PAD))
    spread = np.zeros((4, GROUPS, 4, 2, 2, 2, GROUPS, 2))
    for block in range(4):
        for group in range(GROUPS):
            for part in range(2):
                for focal in range(2):
                    spread[block, group, block, part, focal, part, group, focal] = 1.0
    spread = spread.reshape(4, 256, 64).astype(ml_dtypes.bfloat16)
    return to_time, to_freq, spread, np.ascontiguousarray(spread.transpose(0, 2, 1))


def dot_nt(left, right):
    return lax.dot_general(left, right, (((1,), (1,)), ((), ())), preferred_element_type=F32)


def dot_nn(left, right):
    return jnp.dot(left, right, preferred_element_type=F32)


def complex_pairs(products, mask_row):
    lane = lax.broadcasted_iota(jnp.int32, products.shape, 1)
    half = products.shape[0] // 2
    turned = jnp.concatenate([products[half:], -products[:half]], axis=0)
    ahead = pltpu.roll(turned, BLOCK - 32, 1)
    behind = pltpu.roll(turned, 32, 1)
    swapped = jnp.where(lane % 64 < 32, ahead, -behind)
    return ((products + swapped) * mask_row).astype(BF16)


def column_of(lane):
    return lane // 64


def block_of(shift, slot):
    index = lax.axis_index("rows")
    row, spot = index // RING, index % RING
    row = 1 - row if slot else row
    return row * RING + lax.rem(spot + shift + RING, RING)


def mask_of(ranks, block, i):
    lane = lax.broadcasted_iota(jnp.int32, (1, BLOCK), 1)
    rank = jnp.full((1, BLOCK), ranks[i, 4 * block], jnp.int32)
    for t in range(1, 4):
        rank = jnp.where(column_of(lane) == t, ranks[i, 4 * block + t], rank)
    return jnp.where(lane % 32 < rank, 1.0, 0.0)


def rows_of(block):
    return pl.ds(pl.multiple_of(block * BLOCK, BLOCK), BLOCK)


def forward_kernel(targets, has_start, last, ranks, *refs):
    count = len(targets)
    chunks, refs = refs[:count], refs[count:]
    right, left, refs = refs[0], refs[1], refs[2:]
    start, spread = None, None
    if has_start:
        start, refs = refs[0], refs[1:]
    if last:
        spread, refs = refs[0], refs[1:]
    out = refs[0]
    lane = lax.broadcasted_iota(jnp.int32, (64, BLOCK), 1)
    totals = [start[:, 256 * i : 256 * i + 256] if has_start else None for i in range(2)]
    for n in range(count):
        for at, (shift, slot) in enumerate(targets[n]):
            block = block_of(shift, slot)
            rows = rows_of(block)
            stacked = jnp.concatenate(
                [chunks[n][at, :, 256 * t : 256 * t + 256] for t in range(4)], axis=0
            )
            for i in range(2):
                products = dot_nt(stacked, right[i, rows, :])
                mine = products[0:64]
                for t in range(1, 4):
                    mine = jnp.where(column_of(lane) == t, products[64 * t : 64 * t + 64], mine)
                coefficients = complex_pairs(mine, mask_of(ranks, block, i))
                part = dot_nn(coefficients, left[i, rows, :])
                totals[i] = part if totals[i] is None else totals[i] + part
    if last:
        rounded = [total.astype(BF16) for total in totals]
        moved = None
        for b in range(4):
            piece = dot_nn(spread[b], rounded[b // 2][:, 128 * (b % 2) : 128 * (b % 2) + 128])
            moved = piece if moved is None else moved + piece
        out[...] = moved.astype(BF16).reshape(GROUPS, 16, 128)
    else:
        for i in range(2):
            out[:, 256 * i : 256 * i + 256] = totals[i]


def params():
    return pltpu.CompilerParams(vmem_limit_bytes=24 * 1024 * 1024)


def cost(columns):
    return pl.CostEstimate(
        flops=2 * columns * 10_000_000, bytes_accessed=columns * 150_000, transcendentals=0
    )


def both(shift):
    return ((shift, 0), (shift, 1))


FAR = (((HALF, 0),), ((HALF, 1),))
INDEX = pl.BlockSpec(memory_space=pltpu.SMEM)
LOCAL = pl.BlockSpec(memory_space=pltpu.VMEM)


def forward_part(chunks, targets, ranks, right, left, start=None, spread=None):
    columns = 4 * sum(len(target) for target in targets)
    last = spread is not None
    operands = list(chunks) + [right, left]
    if start is not None:
        operands.append(start)
    if last:
        operands.append(spread)
        out_shape = jax.ShapeDtypeStruct((GROUPS, 16, 128), BF16)
    else:
        out_shape = jax.ShapeDtypeStruct((64, 512), F32)
    return pl.pallas_call(
        functools.partial(forward_kernel, targets, start is not None, last),
        in_specs=[INDEX] + [LOCAL] * len(operands),
        out_specs=LOCAL,
        out_shape=out_shape,
        compiler_params=params(),
        cost_estimate=cost(columns),
        name="forward_part",
    )(ranks, *operands)


def adjoint_kernel(targets, first, ranks, *refs):
    count = len(targets)
    field, refs = refs[0], refs[1:]
    gather = None
    if first:
        gather, refs = refs[0], refs[1:]
    right, left, refs = refs[0], refs[1], refs[2:]
    outs, refs = refs[:count], refs[count:]
    if first:
        natural = refs[0]
        received = field[...].reshape(256, 128)
        pieces = [dot_nn(gather[b], received).astype(BF16) for b in range(4)]
        for b in range(4):
            natural[:, 128 * b : 128 * b + 128] = pieces[b]
        halves = [jnp.concatenate(pieces[2 * i : 2 * i + 2], axis=1) for i in range(2)]
    else:
        halves = [field[:, 256 * i : 256 * i + 256] for i in range(2)]
    lane = lax.broadcasted_iota(jnp.int32, (64, BLOCK), 1)
    for n in range(count):
        for at, (shift, slot) in enumerate(targets[n]):
            block = block_of(shift, slot)
            rows = rows_of(block)
            sums = None
            for i in range(2):
                products = dot_nt(halves[i], left[i, rows, :])
                coefficients = complex_pairs(products, mask_of(ranks, block, i))
                none = jnp.zeros_like(coefficients)
                spread = jnp.concatenate(
                    [jnp.where(column_of(lane) == t, coefficients, none) for t in range(4)], axis=0
                )
                part = dot_nn(spread, right[i, rows, :])
                sums = part if sums is None else sums + part
            sums = sums.astype(BF16)
            for t in range(4):
                outs[n][at, :, 256 * t : 256 * t + 256] = sums[64 * t : 64 * t + 64]


def adjoint_part(field, targets, ranks, right, left, gather=None):
    columns = 4 * sum(len(target) for target in targets)
    first = gather is not None
    operands = [field] + ([gather] if first else []) + [right, left]
    out_shape = [jax.ShapeDtypeStruct((len(target), 64, 1024), BF16) for target in targets]
    if first:
        out_shape.append(jax.ShapeDtypeStruct((64, 512), BF16))
    return pl.pallas_call(
        functools.partial(adjoint_kernel, targets, first),
        in_specs=[INDEX] + [LOCAL] * len(operands),
        out_specs=[LOCAL] * len(out_shape),
        out_shape=out_shape,
        compiler_params=params(),
        cost_estimate=cost(columns),
        name="adjoint_part",
    )(ranks, *operands)


def stack_kernel(own, other, out):
    out[0] = own[...]
    out[1] = other[...]


def stack_pair(own, other):
    return pl.pallas_call(
        stack_kernel,
        in_specs=[LOCAL, LOCAL],
        out_specs=LOCAL,
        out_shape=jax.ShapeDtypeStruct((2,) + own.shape, own.dtype),
        compiler_params=params(),
        name="stack_pair",
    )(own, other)


def window_kernel(field, onset, to_time, to_freq, out):
    received = field[...].reshape(256, 128)
    signal = dot_nn(to_time[0], received) + dot_nn(to_time[1], received)
    signal = signal.reshape(8, SAMPLE_PAD, 128)
    time = lax.broadcasted_iota(jnp.int32, signal.shape, 1)
    kept = jnp.where(time < onset[...][:, None, :], signal, 0.0).reshape(8 * SAMPLE_PAD, 128)
    high = kept.astype(BF16)
    low = (kept - high.astype(F32)).astype(BF16)
    back = dot_nn(to_freq[0], high) + dot_nn(to_freq[1], high) + dot_nn(to_freq[0], low)
    out[...] = back.astype(BF16).reshape(GROUPS, 16, 128)


def window_block(field, onset, to_time, to_freq):
    return pl.pallas_call(
        window_kernel,
        out_shape=jax.ShapeDtypeStruct((GROUPS, 16, 128), BF16),
        compiler_params=pltpu.CompilerParams(vmem_limit_bytes=16 * 1024 * 1024),
        cost_estimate=pl.CostEstimate(flops=200_000_000, bytes_accessed=1_000_000, transcendentals=0),
        name="window",
    )(field, onset, to_time, to_freq)


def exchange(value):
    return lax.all_to_all(value, "freq", split_axis=0, concat_axis=0, tiled=True)


def add(*terms):
    total = terms[0].astype(F32)
    for term in terms[1:]:
        total = total + term.astype(F32)
    return total.astype(BF16)


def on_device(left_factors, right_factors, tile_ranks, window_onset, direct_wave):
    left = pltpu.with_memory_space_constraint(left_factors.reshape(2, 4096, 256), pltpu.VMEM)
    right = pltpu.with_memory_space_constraint(right_factors.reshape(2, 4096, 256), pltpu.VMEM)
    ranks = tile_ranks.reshape(2, 64)
    onset = jnp.transpose(window_onset.reshape(4, 128, 2), (0, 2, 1)).reshape(8, 128)
    to_time, to_freq, spread, gather = [jnp.asarray(table) for table in tables()]

    direct = direct_wave.reshape(64, 1024)
    direct_pair = stack_pair(direct, permute(direct, ACROSS))
    pair = direct_pair
    minus_field = None
    current = None
    for iteration in range(ITERS):
        total = forward_part([pair], [both(0)], ranks, right, left)
        up, down = permute(pair, UP), permute(pair, DOWN)
        for step in range(1, HALF):
            held = (up, down)
            last = step == HALF - 1
            up, total = lax.optimization_barrier((up, total))
            up = permute(up[0:1] if last else up, UP)
            down = permute(down[1:2] if last else down, DOWN)
            total = forward_part(held, [both(-step), both(step)], ranks, right, left, start=total)
        far = (up, down)
        reflected = forward_part(
            far, FAR, ranks, right, left, start=total, spread=spread
        )
        windowed = window_block(exchange(reflected), onset, to_time, to_freq)
        received = exchange(windowed)
        far_first, far_second, minus_field = adjoint_part(
            received, FAR, ranks, right, left, gather=gather
        )
        up, down = permute(far_first, UP), permute(far_second, DOWN)
        for step in range(HALF - 1, 0, -1):
            to_up, to_down = adjoint_part(minus_field, [both(step), both(-step)], ranks, right, left)
            if step == HALF - 1:
                to_up = jnp.concatenate([add(to_up[0:1], up), to_up[1:2]], axis=0)
                to_down = jnp.concatenate([to_down[0:1], add(to_down[1:2], down)], axis=0)
            else:
                to_up, to_down = add(to_up, up), add(to_down, down)
            up, down = permute(to_up, UP), permute(to_down, DOWN)
        (own,) = adjoint_part(minus_field, [both(0)], ranks, right, left)
        if iteration < ITERS - 1:
            summed = add(own, up, down)
            other = permute(summed, ACROSS)
            pair = add(direct_pair, summed, other[::-1])
        else:
            other = permute(add(own[1], up[1], down[1]), ACROSS)
            current = add(direct, own[0], up[0], down[0], other)
    return (current.reshape(1, 2, 32, 1024), minus_field.reshape(1, 2, 32, 512))


def solution(mesh):
    in_specs = (
        P("freq", "rows", None, None, None, None),
        P("freq", "rows", None, None, None, None),
        P("freq", "rows", None),
        P("rows", "freq"),
        P("freq", None, None, "rows"),
    )
    out_specs = (P("freq", None, None, "rows"), P("freq", None, None, "rows"))
    return jax.shard_map(
        on_device, mesh=mesh, in_specs=in_specs, out_specs=out_specs, check_vma=False
    )
```

```python
import functools
import math

import jax
import jax.numpy as jnp
import ml_dtypes
import numpy as np
from jax import lax
from jax.experimental import pallas as pl
from jax.experimental.pallas import tpu as pltpu
from jax.sharding import PartitionSpec as P

ITERS = 2
RING = 8
HALF = RING // 2
BLOCK = 256
GROUPS = 16
SAMPLES = 34
SAMPLE_PAD = 40
F32 = jnp.float32
BF16 = jnp.bfloat16

UP = [(y * RING + z, y * RING + (z + 1) % RING) for y in range(2) for z in range(RING)]
DOWN = [(b, a) for a, b in UP]
ACROSS = [(r, (r + RING) % (2 * RING)) for r in range(2 * RING)]


def permute(value, pairs):
    return lax.ppermute(value, "rows", pairs)


def split_table(table):
    high = table.astype(ml_dtypes.bfloat16)
    low = (table - high.astype(np.float64)).astype(ml_dtypes.bfloat16)
    return np.stack([high, low])


def tables():
    bins = np.arange(GROUPS) + 1
    times = np.arange(SAMPLES)
    angle = 2.0 * math.pi * ((bins[:, None] * times[None, :]) % SAMPLES) / SAMPLES
    norm = 1.0 / math.sqrt(GROUPS + 1)
    cos_table, sin_table = norm * np.cos(angle), norm * np.sin(angle)
    to_time = np.zeros((4, 2, SAMPLE_PAD, GROUPS, 4, 2, 2))
    to_freq = np.zeros((GROUPS, 4, 2, 2, 4, 2, SAMPLE_PAD))
    for block in range(4):
        for focal in range(2):
            to_time[block, focal, :SAMPLES, :, block, 0, focal] = cos_table.T
            to_time[block, focal, :SAMPLES, :, block, 1, focal] = -sin_table.T
            to_freq[:, block, 0, focal, block, focal, :SAMPLES] = cos_table
            to_freq[:, block, 1, focal, block, focal, :SAMPLES] = -sin_table
    to_time = split_table(to_time.reshape(8 * SAMPLE_PAD, 256))
    to_freq = split_table(to_freq.reshape(256, 8 * SAMPLE_PAD))
    spread = np.zeros((4, GROUPS, 4, 2, 2, 2, GROUPS, 2))
    for block in range(4):
        for group in range(GROUPS):
            for part in range(2):
                for focal in range(2):
                    spread[block, group, block, part, focal, part, group, focal] = 1.0
    spread = spread.reshape(4, 256, 64).astype(ml_dtypes.bfloat16)
    return to_time, to_freq, spread, np.ascontiguousarray(spread.transpose(0, 2, 1))


def dot_nt(left, right):
    return lax.dot_general(left, right, (((1,), (1,)), ((), ())), preferred_element_type=F32)


def dot_nn(left, right):
    return jnp.dot(left, right, preferred_element_type=F32)


def complex_pairs(products, mask_row):
    lane = lax.broadcasted_iota(jnp.int32, products.shape, 1)
    half = products.shape[0] // 2
    turned = jnp.concatenate([products[half:], -products[:half]], axis=0)
    ahead = pltpu.roll(turned, BLOCK - 32, 1)
    behind = pltpu.roll(turned, 32, 1)
    swapped = jnp.where(lane % 64 < 32, ahead, -behind)
    return ((products + swapped) * mask_row).astype(BF16)


def column_of(lane):
    return lane // 64


def block_of(shift, slot):
    index = lax.axis_index("rows")
    row, spot = index // RING, index % RING
    row = 1 - row if slot else row
    return row * RING + lax.rem(spot + shift + RING, RING)


def mask_of(ranks, block, i):
    lane = lax.broadcasted_iota(jnp.int32, (1, BLOCK), 1)
    rank = jnp.full((1, BLOCK), ranks[i, 4 * block], jnp.int32)
    for t in range(1, 4):
        rank = jnp.where(column_of(lane) == t, ranks[i, 4 * block + t], rank)
    return jnp.where(lane % 32 < rank, 1.0, 0.0)


def rows_of(block):
    return pl.ds(pl.multiple_of(block * BLOCK, BLOCK), BLOCK)


def stack_columns(chunk):
    return jnp.concatenate([chunk[:, 256 * t : 256 * t + 256] for t in range(4)], axis=0)


def forward_coefficients(stacked, right_rows, mask_row):
    products = dot_nt(stacked, right_rows)
    lane = lax.broadcasted_iota(jnp.int32, (64, BLOCK), 1)
    mine = products[0:64]
    for t in range(1, 4):
        mine = jnp.where(column_of(lane) == t, products[64 * t : 64 * t + 64], mine)
    return complex_pairs(mine, mask_row)


def forward_kernel(targets, has_start, last, ranks, *refs):
    count = len(targets)
    chunks, refs = refs[:count], refs[count:]
    right, left, refs = refs[0], refs[1], refs[2:]
    start, spread = None, None
    if has_start:
        start, refs = refs[0], refs[1:]
    if last:
        spread, refs = refs[0], refs[1:]
    out = refs[0]
    totals = [start[:, 256 * i : 256 * i + 256] if has_start else None for i in range(2)]
    for chunk, (shift, slot) in zip(chunks, targets):
        block = block_of(shift, slot)
        rows = rows_of(block)
        stacked = stack_columns(chunk)
        for i in range(2):
            coefficients = forward_coefficients(stacked, right[i, rows, :], mask_of(ranks, block, i))
            part = dot_nn(coefficients, left[i, rows, :])
            totals[i] = part if totals[i] is None else totals[i] + part
    if last:
        rounded = [total.astype(BF16) for total in totals]
        moved = None
        for b in range(4):
            piece = dot_nn(spread[b], rounded[b // 2][:, 128 * (b % 2) : 128 * (b % 2) + 128])
            moved = piece if moved is None else moved + piece
        out[...] = moved.astype(BF16).reshape(GROUPS, 16, 128)
    else:
        for i in range(2):
            out[:, 256 * i : 256 * i + 256] = totals[i]


def params():
    return pltpu.CompilerParams(vmem_limit_bytes=24 * 1024 * 1024)


def cost(columns):
    return pl.CostEstimate(
        flops=2 * columns * 10_000_000, bytes_accessed=columns * 150_000, transcendentals=0
    )


OWN = ((0, 0), (0, 1))
FAR = ((HALF, 0), (HALF, 1))


def ring_targets(step):
    return ((-step, 0), (step, 0), (-step, 1), (step, 1))


INDEX = pl.BlockSpec(memory_space=pltpu.SMEM)
LOCAL = pl.BlockSpec(memory_space=pltpu.VMEM)


def opening_kernel(targets, ranks, own, other, right, left, out, rights, lefts, arrived):
    copies = []
    for at, (shift, slot) in enumerate(targets):
        rows = rows_of(block_of(shift, slot))
        for kind, (source, room) in enumerate(((right, rights), (left, lefts))):
            copy = pltpu.make_async_copy(source.at[:, rows, :], room.at[at], arrived.at[at, kind])
            copy.start()
            copies.append(copy)
    totals = [None, None]
    for at, (shift, slot) in enumerate(targets):
        block = block_of(shift, slot)
        stacked = stack_columns((own, other)[at])
        copies[2 * at].wait()
        coefficients = [
            forward_coefficients(stacked, rights[at, i], mask_of(ranks, block, i)) for i in range(2)
        ]
        copies[2 * at + 1].wait()
        for i in range(2):
            part = dot_nn(coefficients[i], lefts[at, i])
            totals[i] = part if totals[i] is None else totals[i] + part
    for i in range(2):
        out[:, 256 * i : 256 * i + 256] = totals[i]


def opening_part(chunks, targets, ranks, right, left):
    slots = len(targets)
    stored = [pltpu.with_memory_space_constraint(factors, pltpu.HBM) for factors in (right, left)]
    return pl.pallas_call(
        functools.partial(opening_kernel, targets),
        in_specs=[INDEX, LOCAL, LOCAL] + [pl.BlockSpec(memory_space=pl.ANY)] * 2,
        out_specs=LOCAL,
        out_shape=jax.ShapeDtypeStruct((64, 512), F32),
        scratch_shapes=[
            pltpu.VMEM((slots, 2, BLOCK, 256), BF16),
            pltpu.VMEM((slots, 2, BLOCK, 256), BF16),
            pltpu.SemaphoreType.DMA((slots, 2)),
        ],
        compiler_params=params(),
        cost_estimate=cost(4 * slots),
        name="opening_part",
    )(ranks, *chunks, *stored)


def forward_part(chunks, targets, ranks, right, left, start=None, spread=None):
    columns = 4 * len(targets)
    last = spread is not None
    operands = list(chunks) + [right, left]
    if start is not None:
        operands.append(start)
    if last:
        operands.append(spread)
        out_shape = jax.ShapeDtypeStruct((GROUPS, 16, 128), BF16)
    else:
        out_shape = jax.ShapeDtypeStruct((64, 512), F32)
    return pl.pallas_call(
        functools.partial(forward_kernel, targets, start is not None, last),
        in_specs=[INDEX] + [LOCAL] * len(operands),
        out_specs=LOCAL,
        out_shape=out_shape,
        compiler_params=params(),
        cost_estimate=cost(columns),
        name="forward_part",
    )(ranks, *operands)


def adjoint_kernel(targets, first, ranks, *refs):
    count = len(targets)
    field, refs = refs[0], refs[1:]
    gather = None
    if first:
        gather, refs = refs[0], refs[1:]
    right, left, refs = refs[0], refs[1], refs[2:]
    outs, refs = refs[:count], refs[count:]
    if first:
        natural = refs[0]
        received = field[...].reshape(256, 128)
        pieces = [dot_nn(gather[b], received).astype(BF16) for b in range(4)]
        for b in range(4):
            natural[:, 128 * b : 128 * b + 128] = pieces[b]
        halves = [jnp.concatenate(pieces[2 * i : 2 * i + 2], axis=1) for i in range(2)]
    else:
        halves = [field[:, 256 * i : 256 * i + 256] for i in range(2)]
    lane = lax.broadcasted_iota(jnp.int32, (64, BLOCK), 1)
    for out, (shift, slot) in zip(outs, targets):
        block = block_of(shift, slot)
        rows = rows_of(block)
        sums = None
        for i in range(2):
            products = dot_nt(halves[i], left[i, rows, :])
            coefficients = complex_pairs(products, mask_of(ranks, block, i))
            none = jnp.zeros_like(coefficients)
            spread = jnp.concatenate(
                [jnp.where(column_of(lane) == t, coefficients, none) for t in range(4)], axis=0
            )
            part = dot_nn(spread, right[i, rows, :])
            sums = part if sums is None else sums + part
        sums = sums.astype(BF16)
        for t in range(4):
            out[:, 256 * t : 256 * t + 256] = sums[64 * t : 64 * t + 64]


def adjoint_part(field, targets, ranks, right, left, gather=None):
    columns = 4 * len(targets)
    first = gather is not None
    operands = [field] + ([gather] if first else []) + [right, left]
    out_shape = [jax.ShapeDtypeStruct((64, 1024), BF16)] * len(targets)
    if first:
        out_shape.append(jax.ShapeDtypeStruct((64, 512), BF16))
    return pl.pallas_call(
        functools.partial(adjoint_kernel, targets, first),
        in_specs=[INDEX] + [LOCAL] * len(operands),
        out_specs=[LOCAL] * len(out_shape),
        out_shape=out_shape,
        compiler_params=params(),
        cost_estimate=cost(columns),
        name="adjoint_part",
    )(ranks, *operands)


def window_kernel(field, onset, to_time, to_freq, out):
    received = field[...].reshape(256, 128)
    signal = dot_nn(to_time[0], received) + dot_nn(to_time[1], received)
    signal = signal.reshape(8, SAMPLE_PAD, 128)
    time = lax.broadcasted_iota(jnp.int32, signal.shape, 1)
    kept = jnp.where(time < onset[...][:, None, :], signal, 0.0).reshape(8 * SAMPLE_PAD, 128)
    high = kept.astype(BF16)
    low = (kept - high.astype(F32)).astype(BF16)
    back = dot_nn(to_freq[0], high) + dot_nn(to_freq[1], high) + dot_nn(to_freq[0], low)
    out[...] = back.astype(BF16).reshape(GROUPS, 16, 128)


def window_block(field, onset, to_time, to_freq):
    return pl.pallas_call(
        window_kernel,
        out_shape=jax.ShapeDtypeStruct((GROUPS, 16, 128), BF16),
        compiler_params=pltpu.CompilerParams(vmem_limit_bytes=16 * 1024 * 1024),
        cost_estimate=pl.CostEstimate(flops=200_000_000, bytes_accessed=1_000_000, transcendentals=0),
        name="window",
    )(field, onset, to_time, to_freq)


def exchange(value):
    return lax.all_to_all(value, "freq", split_axis=0, concat_axis=0, tiled=True)


def add(*terms):
    total = terms[0].astype(F32)
    for term in terms[1:]:
        total = total + term.astype(F32)
    return total.astype(BF16)


def on_device(left_factors, right_factors, tile_ranks, window_onset, direct_wave):
    left = left_factors.reshape(2, 4096, 256)
    right = right_factors.reshape(2, 4096, 256)
    ranks = tile_ranks.reshape(2, 64)
    onset = jnp.transpose(window_onset.reshape(4, 128, 2), (0, 2, 1)).reshape(8, 128)
    to_time, to_freq, spread, gather = [jnp.asarray(table) for table in tables()]

    direct = direct_wave.reshape(64, 1024)
    direct_other = permute(direct, ACROSS)
    own, other = direct, direct_other
    minus_field = None
    current = None
    for iteration in range(ITERS):
        opening = opening_part if iteration == 0 else forward_part
        total = opening([own, other], OWN, ranks, right, left)
        streams = [permute(own, UP), permute(own, DOWN), permute(other, UP), permute(other, DOWN)]
        for step in range(1, HALF):
            held = list(streams)
            streams[0], total = lax.optimization_barrier((streams[0], total))
            if step < HALF - 1:
                streams = [permute(chunk, (UP, DOWN)[n % 2]) for n, chunk in enumerate(streams)]
            else:
                streams = [permute(streams[0], UP), permute(streams[3], DOWN)]
            total = forward_part(held, ring_targets(step), ranks, right, left, start=total)
        reflected = forward_part(streams, FAR, ranks, right, left, start=total, spread=spread)
        windowed = window_block(exchange(reflected), onset, to_time, to_freq)
        received = exchange(windowed)
        far_own, far_other, minus_field = adjoint_part(received, FAR, ranks, right, left, gather=gather)
        field = minus_field
        coming = [permute(far_own, UP), None, None, permute(far_other, DOWN)]
        for step in range(HALF - 1, 0, -1):
            terms = adjoint_part(field, ring_targets(-step), ranks, right, left)
            terms = [term if came is None else add(term, came) for term, came in zip(terms, coming)]
            coming = [permute(term, (UP, DOWN)[n % 2]) for n, term in enumerate(terms)]
            field, _ = lax.optimization_barrier((field, terms[0]))
        own_term, other_term = adjoint_part(field, OWN, ranks, right, left)
        other_sum = add(other_term, coming[2], coming[3])
        own_sum = add(own_term, coming[0], coming[1])
        own = add(direct, own_sum, permute(other_sum, ACROSS))
        if iteration < ITERS - 1:
            other = add(direct_other, other_sum, permute(own_sum, ACROSS))
        else:
            current = own
    return (current.reshape(1, 2, 32, 1024), minus_field.reshape(1, 2, 32, 512))


def solution(mesh):
    in_specs = (
        P("freq", "rows", None, None, None, None),
        P("freq", "rows", None, None, None, None),
        P("freq", "rows", None),
        P("rows", "freq"),
        P("freq", None, None, "rows"),
    )
    out_specs = (P("freq", None, None, "rows"), P("freq", None, None, "rows"))
    return jax.shard_map(
        on_device, mesh=mesh, in_specs=in_specs, out_specs=out_specs, check_vma=False
    )
```

```python
import functools
import math

import jax
import jax.numpy as jnp
import ml_dtypes
import numpy as np
from jax import lax
from jax.experimental import pallas as pl
from jax.experimental.pallas import tpu as pltpu
from jax.sharding import PartitionSpec as P

ITERS = 2
RING = 8
HALF = RING // 2
BLOCK = 256
GROUPS = 16
SAMPLES = 34
SAMPLE_PAD = 40
F32 = jnp.float32
BF16 = jnp.bfloat16

UP = [(y * RING + z, y * RING + (z + 1) % RING) for y in range(2) for z in range(RING)]
DOWN = [(b, a) for a, b in UP]
ACROSS = [(r, (r + RING) % (2 * RING)) for r in range(2 * RING)]


def permute(value, pairs):
    return lax.ppermute(value, "rows", pairs)


def split_table(table):
    high = table.astype(ml_dtypes.bfloat16)
    low = (table - high.astype(np.float64)).astype(ml_dtypes.bfloat16)
    return np.stack([high, low])


def tables():
    bins = np.arange(GROUPS) + 1
    times = np.arange(SAMPLES)
    angle = 2.0 * math.pi * ((bins[:, None] * times[None, :]) % SAMPLES) / SAMPLES
    norm = 1.0 / math.sqrt(GROUPS + 1)
    cos_table, sin_table = norm * np.cos(angle), norm * np.sin(angle)
    to_time = np.zeros((4, 2, SAMPLE_PAD, GROUPS, 4, 2, 2))
    to_freq = np.zeros((GROUPS, 4, 2, 2, 4, 2, SAMPLE_PAD))
    for block in range(4):
        for focal in range(2):
            to_time[block, focal, :SAMPLES, :, block, 0, focal] = cos_table.T
            to_time[block, focal, :SAMPLES, :, block, 1, focal] = -sin_table.T
            to_freq[:, block, 0, focal, block, focal, :SAMPLES] = cos_table
            to_freq[:, block, 1, focal, block, focal, :SAMPLES] = -sin_table
    to_time = split_table(to_time.reshape(8 * SAMPLE_PAD, 256))
    to_freq = split_table(to_freq.reshape(256, 8 * SAMPLE_PAD))
    spread = np.zeros((4, GROUPS, 4, 2, 2, 2, GROUPS, 2))
    for block in range(4):
        for group in range(GROUPS):
            for part in range(2):
                for focal in range(2):
                    spread[block, group, block, part, focal, part, group, focal] = 1.0
    spread = spread.reshape(4, 256, 64).astype(ml_dtypes.bfloat16)
    return to_time, to_freq, spread, np.ascontiguousarray(spread.transpose(0, 2, 1))


def dot_nt(left, right):
    return lax.dot_general(left, right, (((1,), (1,)), ((), ())), preferred_element_type=F32)


def dot_nn(left, right):
    return jnp.dot(left, right, preferred_element_type=F32)


def complex_pairs(products, mask_row):
    lane = lax.broadcasted_iota(jnp.int32, products.shape, 1)
    half = products.shape[0] // 2
    turned = jnp.concatenate([products[half:], -products[:half]], axis=0)
    ahead = pltpu.roll(turned, BLOCK - 32, 1)
    behind = pltpu.roll(turned, 32, 1)
    swapped = jnp.where(lane % 64 < 32, ahead, -behind)
    return ((products + swapped) * mask_row).astype(BF16)


def column_of(lane):
    return lane // 64


def block_of(shift, slot):
    index = lax.axis_index("rows")
    row, spot = index // RING, index % RING
    row = 1 - row if slot else row
    return row * RING + lax.rem(spot + shift + RING, RING)


def mask_of(ranks, block, i):
    lane = lax.broadcasted_iota(jnp.int32, (1, BLOCK), 1)
    rank = jnp.full((1, BLOCK), ranks[i, 4 * block], jnp.int32)
    for t in range(1, 4):
        rank = jnp.where(column_of(lane) == t, ranks[i, 4 * block + t], rank)
    return jnp.where(lane % 32 < rank, 1.0, 0.0)


def rows_of(block):
    return pl.ds(pl.multiple_of(block * BLOCK, BLOCK), BLOCK)


def stack_columns(chunk):
    return jnp.concatenate([chunk[:, 256 * t : 256 * t + 256] for t in range(4)], axis=0)


def forward_coefficients(stacked, right_rows, mask_row):
    products = dot_nt(stacked, right_rows)
    lane = lax.broadcasted_iota(jnp.int32, (64, BLOCK), 1)
    mine = products[0:64]
    for t in range(1, 4):
        mine = jnp.where(column_of(lane) == t, products[64 * t : 64 * t + 64], mine)
    return complex_pairs(mine, mask_row)


def forward_kernel(targets, has_start, last, ranks, *refs):
    count = len(targets)
    chunks, refs = refs[:count], refs[count:]
    right, left, refs = refs[0], refs[1], refs[2:]
    start, spread = None, None
    if has_start:
        start, refs = refs[0], refs[1:]
    if last:
        spread, refs = refs[0], refs[1:]
    out = refs[0]
    totals = [start[:, 256 * i : 256 * i + 256] if has_start else None for i in range(2)]
    for chunk, (shift, slot) in zip(chunks, targets):
        block = block_of(shift, slot)
        rows = rows_of(block)
        stacked = stack_columns(chunk)
        for i in range(2):
            coefficients = forward_coefficients(stacked, right[i, rows, :], mask_of(ranks, block, i))
            part = dot_nn(coefficients, left[i, rows, :])
            totals[i] = part if totals[i] is None else totals[i] + part
    if last:
        rounded = [total.astype(BF16) for total in totals]
        moved = None
        for b in range(4):
            piece = dot_nn(spread[b], rounded[b // 2][:, 128 * (b % 2) : 128 * (b % 2) + 128])
            moved = piece if moved is None else moved + piece
        out[...] = moved.astype(BF16).reshape(GROUPS, 16, 128)
    else:
        for i in range(2):
            out[:, 256 * i : 256 * i + 256] = totals[i]


def params():
    return pltpu.CompilerParams(vmem_limit_bytes=24 * 1024 * 1024)


def cost(columns):
    return pl.CostEstimate(
        flops=2 * columns * 10_000_000, bytes_accessed=columns * 150_000, transcendentals=0
    )


OWN = ((0, 0), (0, 1))
FAR = ((HALF, 0), (HALF, 1))


def ring_targets(step):
    return ((-step, 0), (step, 0), (-step, 1), (step, 1))


INDEX = pl.BlockSpec(memory_space=pltpu.SMEM)
LOCAL = pl.BlockSpec(memory_space=pltpu.VMEM)


def opening_kernel(targets, ranks, own, right, left, out, rights, lefts, arrived):
    copies = []
    for at, (shift, slot) in enumerate(targets):
        rows = rows_of(block_of(shift, slot))
        for kind, (source, room) in enumerate(((right, rights), (left, lefts))):
            copy = pltpu.make_async_copy(source.at[:, rows, :], room.at[at], arrived.at[at, kind])
            copy.start()
            copies.append(copy)
    totals = [None, None]
    for at, (shift, slot) in enumerate(targets):
        block = block_of(shift, slot)
        stacked = stack_columns((own,)[at])
        copies[2 * at].wait()
        coefficients = [
            forward_coefficients(stacked, rights[at, i], mask_of(ranks, block, i)) for i in range(2)
        ]
        copies[2 * at + 1].wait()
        for i in range(2):
            part = dot_nn(coefficients[i], lefts[at, i])
            totals[i] = part if totals[i] is None else totals[i] + part
    for i in range(2):
        out[:, 256 * i : 256 * i + 256] = totals[i]


def opening_part(chunks, targets, ranks, right, left):
    slots = len(targets)
    stored = [pltpu.with_memory_space_constraint(factors, pltpu.HBM) for factors in (right, left)]
    return pl.pallas_call(
        functools.partial(opening_kernel, targets),
        in_specs=[INDEX, LOCAL] + [pl.BlockSpec(memory_space=pl.ANY)] * 2,
        out_specs=LOCAL,
        out_shape=jax.ShapeDtypeStruct((64, 512), F32),
        scratch_shapes=[
            pltpu.VMEM((slots, 2, BLOCK, 256), BF16),
            pltpu.VMEM((slots, 2, BLOCK, 256), BF16),
            pltpu.SemaphoreType.DMA((slots, 2)),
        ],
        compiler_params=params(),
        cost_estimate=cost(4 * slots),
        name="opening_part",
    )(ranks, *chunks, *stored)


def forward_part(chunks, targets, ranks, right, left, start=None, spread=None):
    columns = 4 * len(targets)
    last = spread is not None
    operands = list(chunks) + [right, left]
    if start is not None:
        operands.append(start)
    if last:
        operands.append(spread)
        out_shape = jax.ShapeDtypeStruct((GROUPS, 16, 128), BF16)
    else:
        out_shape = jax.ShapeDtypeStruct((64, 512), F32)
    return pl.pallas_call(
        functools.partial(forward_kernel, targets, start is not None, last),
        in_specs=[INDEX] + [LOCAL] * len(operands),
        out_specs=LOCAL,
        out_shape=out_shape,
        compiler_params=params(),
        cost_estimate=cost(columns),
        name="forward_part",
    )(ranks, *operands)


def adjoint_kernel(targets, first, ranks, *refs):
    count = len(targets)
    field, refs = refs[0], refs[1:]
    gather = None
    if first:
        gather, refs = refs[0], refs[1:]
    right, left, refs = refs[0], refs[1], refs[2:]
    outs, refs = refs[:count], refs[count:]
    if first:
        natural = refs[0]
        received = field[...].reshape(256, 128)
        pieces = [dot_nn(gather[b], received).astype(BF16) for b in range(4)]
        for b in range(4):
            natural[:, 128 * b : 128 * b + 128] = pieces[b]
        halves = [jnp.concatenate(pieces[2 * i : 2 * i + 2], axis=1) for i in range(2)]
    else:
        halves = [field[:, 256 * i : 256 * i + 256] for i in range(2)]
    lane = lax.broadcasted_iota(jnp.int32, (64, BLOCK), 1)
    for out, (shift, slot) in zip(outs, targets):
        block = block_of(shift, slot)
        rows = rows_of(block)
        sums = None
        for i in range(2):
            products = dot_nt(halves[i], left[i, rows, :])
            coefficients = complex_pairs(products, mask_of(ranks, block, i))
            none = jnp.zeros_like(coefficients)
            spread = jnp.concatenate(
                [jnp.where(column_of(lane) == t, coefficients, none) for t in range(4)], axis=0
            )
            part = dot_nn(spread, right[i, rows, :])
            sums = part if sums is None else sums + part
        sums = sums.astype(BF16)
        for t in range(4):
            out[:, 256 * t : 256 * t + 256] = sums[64 * t : 64 * t + 64]


def adjoint_part(field, targets, ranks, right, left, gather=None):
    columns = 4 * len(targets)
    first = gather is not None
    operands = [field] + ([gather] if first else []) + [right, left]
    out_shape = [jax.ShapeDtypeStruct((64, 1024), BF16)] * len(targets)
    if first:
        out_shape.append(jax.ShapeDtypeStruct((64, 512), BF16))
    return pl.pallas_call(
        functools.partial(adjoint_kernel, targets, first),
        in_specs=[INDEX] + [LOCAL] * len(operands),
        out_specs=[LOCAL] * len(out_shape),
        out_shape=out_shape,
        compiler_params=params(),
        cost_estimate=cost(columns),
        name="adjoint_part",
    )(ranks, *operands)


def window_kernel(field, onset, to_time, to_freq, out):
    received = field[...].reshape(256, 128)
    signal = dot_nn(to_time[0], received) + dot_nn(to_time[1], received)
    signal = signal.reshape(8, SAMPLE_PAD, 128)
    time = lax.broadcasted_iota(jnp.int32, signal.shape, 1)
    kept = jnp.where(time < onset[...][:, None, :], signal, 0.0).reshape(8 * SAMPLE_PAD, 128)
    high = kept.astype(BF16)
    low = (kept - high.astype(F32)).astype(BF16)
    back = dot_nn(to_freq[0], high) + dot_nn(to_freq[1], high) + dot_nn(to_freq[0], low)
    out[...] = back.astype(BF16).reshape(GROUPS, 16, 128)


def window_block(field, onset, to_time, to_freq):
    return pl.pallas_call(
        window_kernel,
        out_shape=jax.ShapeDtypeStruct((GROUPS, 16, 128), BF16),
        compiler_params=pltpu.CompilerParams(vmem_limit_bytes=16 * 1024 * 1024),
        cost_estimate=pl.CostEstimate(flops=200_000_000, bytes_accessed=1_000_000, transcendentals=0),
        name="window",
    )(field, onset, to_time, to_freq)


def exchange(value):
    return lax.all_to_all(value, "freq", split_axis=0, concat_axis=0, tiled=True)


def add(*terms):
    total = terms[0].astype(F32)
    for term in terms[1:]:
        total = total + term.astype(F32)
    return total.astype(BF16)


def on_device(left_factors, right_factors, tile_ranks, window_onset, direct_wave):
    left = left_factors.reshape(2, 4096, 256)
    right = right_factors.reshape(2, 4096, 256)
    ranks = tile_ranks.reshape(2, 64)
    onset = jnp.transpose(window_onset.reshape(4, 128, 2), (0, 2, 1)).reshape(8, 128)
    to_time, to_freq, spread, gather = [jnp.asarray(table) for table in tables()]

    direct = direct_wave.reshape(64, 1024)
    direct_other = permute(direct, ACROSS)
    own, other = direct, direct_other
    minus_field = None
    current = None
    for iteration in range(ITERS):
        if iteration == 0:
            total = opening_part([own], OWN[:1], ranks, right, left)
            streams = [permute(own, UP), permute(own, DOWN)]
            other, total = lax.optimization_barrier((other, total))
            streams += [permute(other, UP), permute(other, DOWN)]
        else:
            total = forward_part([own, other], OWN, ranks, right, left)
            streams = [permute(own, UP), permute(own, DOWN), permute(other, UP), permute(other, DOWN)]
        for step in range(1, HALF):
            held = list(streams)
            streams[0], total = lax.optimization_barrier((streams[0], total))
            if step < HALF - 1:
                streams = [permute(chunk, (UP, DOWN)[n % 2]) for n, chunk in enumerate(streams)]
            else:
                streams = [permute(streams[0], UP), permute(streams[3], DOWN)]
            targets = ring_targets(step)
            if step == 1 and iteration == 0:
                held, targets = [other] + held, ((0, 1),) + targets
            total = forward_part(held, targets, ranks, right, left, start=total)
        reflected = forward_part(streams, FAR, ranks, right, left, start=total, spread=spread)
        windowed = window_block(exchange(reflected), onset, to_time, to_freq)
        received = exchange(windowed)
        far_own, far_other, minus_field = adjoint_part(received, FAR, ranks, right, left, gather=gather)
        field = minus_field
        coming = [permute(far_own, UP), None, None, permute(far_other, DOWN)]
        for step in range(HALF - 1, 0, -1):
            terms = adjoint_part(field, ring_targets(-step), ranks, right, left)
            terms = [term if came is None else add(term, came) for term, came in zip(terms, coming)]
            coming = [permute(term, (UP, DOWN)[n % 2]) for n, term in enumerate(terms)]
            field, _ = lax.optimization_barrier((field, terms[0]))
        own_term, other_term = adjoint_part(field, OWN, ranks, right, left)
        other_sum = add(other_term, coming[2], coming[3])
        own_sum = add(own_term, coming[0], coming[1])
        own = add(direct, own_sum, permute(other_sum, ACROSS))
        if iteration < ITERS - 1:
            other = add(direct_other, other_sum, permute(own_sum, ACROSS))
        else:
            current = own
    return (current.reshape(1, 2, 32, 1024), minus_field.reshape(1, 2, 32, 512))


def solution(mesh):
    in_specs = (
        P("freq", "rows", None, None, None, None),
        P("freq", "rows", None, None, None, None),
        P("freq", "rows", None),
        P("rows", "freq"),
        P("freq", None, None, "rows"),
    )
    out_specs = (P("freq", None, None, "rows"), P("freq", None, None, "rows"))
    return jax.shard_map(
        on_device, mesh=mesh, in_specs=in_specs, out_specs=out_specs, check_vma=False
    )
```

```python
import functools
import math

import jax
import jax.numpy as jnp
import ml_dtypes
import numpy as np
from jax import lax
from jax.experimental import pallas as pl
from jax.experimental.pallas import tpu as pltpu
from jax.sharding import PartitionSpec as P

ITERS = 2
RING = 8
HALF = RING // 2
BLOCK = 256
GROUPS = 16
SAMPLES = 34
SAMPLE_PAD = 40
F32 = jnp.float32
BF16 = jnp.bfloat16

UP = [(y * RING + z, y * RING + (z + 1) % RING) for y in range(2) for z in range(RING)]
DOWN = [(b, a) for a, b in UP]
ACROSS = [(r, (r + RING) % (2 * RING)) for r in range(2 * RING)]


def permute(value, pairs):
    return lax.ppermute(value, "rows", pairs)


def split_table(table):
    high = table.astype(ml_dtypes.bfloat16)
    low = (table - high.astype(np.float64)).astype(ml_dtypes.bfloat16)
    return np.stack([high, low])


def tables():
    bins = np.arange(GROUPS) + 1
    times = np.arange(SAMPLES)
    angle = 2.0 * math.pi * ((bins[:, None] * times[None, :]) % SAMPLES) / SAMPLES
    norm = 1.0 / math.sqrt(GROUPS + 1)
    cos_table, sin_table = norm * np.cos(angle), norm * np.sin(angle)
    to_time = np.zeros((4, 2, SAMPLE_PAD, GROUPS, 4, 2, 2))
    to_freq = np.zeros((GROUPS, 4, 2, 2, 4, 2, SAMPLE_PAD))
    for block in range(4):
        for focal in range(2):
            to_time[block, focal, :SAMPLES, :, block, 0, focal] = cos_table.T
            to_time[block, focal, :SAMPLES, :, block, 1, focal] = -sin_table.T
            to_freq[:, block, 0, focal, block, focal, :SAMPLES] = cos_table
            to_freq[:, block, 1, focal, block, focal, :SAMPLES] = -sin_table
    to_time = split_table(to_time.reshape(8 * SAMPLE_PAD, 256))
    to_freq = split_table(to_freq.reshape(256, 8 * SAMPLE_PAD))
    spread = np.zeros((4, GROUPS, 4, 2, 2, 2, GROUPS, 2))
    for block in range(4):
        for group in range(GROUPS):
            for part in range(2):
                for focal in range(2):
                    spread[block, group, block, part, focal, part, group, focal] = 1.0
    spread = spread.reshape(4, 256, 64).astype(ml_dtypes.bfloat16)
    return to_time, to_freq, spread, np.ascontiguousarray(spread.transpose(0, 2, 1))


def dot_nt(left, right):
    return lax.dot_general(left, right, (((1,), (1,)), ((), ())), preferred_element_type=F32)


def dot_nn(left, right):
    return jnp.dot(left, right, preferred_element_type=F32)


def complex_pairs(products, mask_row):
    lane = lax.broadcasted_iota(jnp.int32, products.shape, 1)
    half = products.shape[0] // 2
    turned = jnp.concatenate([products[half:], -products[:half]], axis=0)
    ahead = pltpu.roll(turned, BLOCK - 32, 1)
    behind = pltpu.roll(turned, 32, 1)
    swapped = jnp.where(lane % 64 < 32, ahead, -behind)
    return ((products + swapped) * mask_row).astype(BF16)


def column_of(lane):
    return lane // 64


def block_of(shift, slot):
    index = lax.axis_index("rows")
    row, spot = index // RING, index % RING
    row = 1 - row if slot else row
    return row * RING + lax.rem(spot + shift + RING, RING)


def mask_of(ranks, block, i):
    lane = lax.broadcasted_iota(jnp.int32, (1, BLOCK), 1)
    rank = jnp.full((1, BLOCK), ranks[i, 4 * block], jnp.int32)
    for t in range(1, 4):
        rank = jnp.where(column_of(lane) == t, ranks[i, 4 * block + t], rank)
    return jnp.where(lane % 32 < rank, 1.0, 0.0)


def rows_of(block):
    return pl.ds(pl.multiple_of(block * BLOCK, BLOCK), BLOCK)


def stack_columns(chunk):
    return jnp.concatenate([chunk[:, 256 * t : 256 * t + 256] for t in range(4)], axis=0)


def forward_coefficients(stacked, right_rows, mask_row):
    products = dot_nt(stacked, right_rows)
    lane = lax.broadcasted_iota(jnp.int32, (64, BLOCK), 1)
    mine = products[0:64]
    for t in range(1, 4):
        mine = jnp.where(column_of(lane) == t, products[64 * t : 64 * t + 64], mine)
    return complex_pairs(mine, mask_row)


def forward_kernel(targets, has_start, last, ranks, *refs):
    count = len(targets)
    chunks, refs = refs[:count], refs[count:]
    right, left, refs = refs[0], refs[1], refs[2:]
    start, spread = None, None
    if has_start:
        start, refs = refs[0], refs[1:]
    if last:
        spread, refs = refs[0], refs[1:]
    out = refs[0]
    totals = [start[:, 256 * i : 256 * i + 256] if has_start else None for i in range(2)]
    for chunk, (shift, slot) in zip(chunks, targets):
        block = block_of(shift, slot)
        rows = rows_of(block)
        stacked = stack_columns(chunk)
        for i in range(2):
            coefficients = forward_coefficients(stacked, right[i, rows, :], mask_of(ranks, block, i))
            part = dot_nn(coefficients, left[i, rows, :])
            totals[i] = part if totals[i] is None else totals[i] + part
    if last:
        rounded = [total.astype(BF16) for total in totals]
        moved = None
        for b in range(4):
            piece = dot_nn(spread[b], rounded[b // 2][:, 128 * (b % 2) : 128 * (b % 2) + 128])
            moved = piece if moved is None else moved + piece
        out[...] = moved.astype(BF16).reshape(GROUPS, 16, 128)
    else:
        for i in range(2):
            out[:, 256 * i : 256 * i + 256] = totals[i]


def params():
    return pltpu.CompilerParams(vmem_limit_bytes=24 * 1024 * 1024)


def cost(columns):
    return pl.CostEstimate(
        flops=2 * columns * 10_000_000, bytes_accessed=columns * 150_000, transcendentals=0
    )


OWN = ((0, 0), (0, 1))
FAR = ((HALF, 0), (HALF, 1))


def ring_targets(step):
    return ((-step, 0), (step, 0), (-step, 1), (step, 1))


INDEX = pl.BlockSpec(memory_space=pltpu.SMEM)
LOCAL = pl.BlockSpec(memory_space=pltpu.VMEM)


def opening_kernel(targets, ranks, own, right, left, out, rights, lefts, arrived):
    copies = []
    for at, (shift, slot) in enumerate(targets):
        rows = rows_of(block_of(shift, slot))
        for kind, (source, room) in enumerate(((right, rights), (left, lefts))):
            copy = pltpu.make_async_copy(source.at[:, rows, :], room.at[at], arrived.at[at, kind])
            copy.start()
            copies.append(copy)
    totals = [None, None]
    for at, (shift, slot) in enumerate(targets):
        block = block_of(shift, slot)
        stacked = stack_columns((own,)[at])
        copies[2 * at].wait()
        coefficients = [
            forward_coefficients(stacked, rights[at, i], mask_of(ranks, block, i)) for i in range(2)
        ]
        copies[2 * at + 1].wait()
        for i in range(2):
            part = dot_nn(coefficients[i], lefts[at, i])
            totals[i] = part if totals[i] is None else totals[i] + part
    for i in range(2):
        out[:, 256 * i : 256 * i + 256] = totals[i]


def opening_part(chunks, targets, ranks, right, left):
    slots = len(targets)
    stored = [pltpu.with_memory_space_constraint(factors, pltpu.HBM) for factors in (right, left)]
    return pl.pallas_call(
        functools.partial(opening_kernel, targets),
        in_specs=[INDEX, LOCAL] + [pl.BlockSpec(memory_space=pl.ANY)] * 2,
        out_specs=LOCAL,
        out_shape=jax.ShapeDtypeStruct((64, 512), F32),
        scratch_shapes=[
            pltpu.VMEM((slots, 2, BLOCK, 256), BF16),
            pltpu.VMEM((slots, 2, BLOCK, 256), BF16),
            pltpu.SemaphoreType.DMA((slots, 2)),
        ],
        compiler_params=params(),
        cost_estimate=cost(4 * slots),
        name="opening_part",
    )(ranks, *chunks, *stored)


def forward_part(chunks, targets, ranks, right, left, start=None, spread=None):
    columns = 4 * len(targets)
    last = spread is not None
    operands = list(chunks) + [right, left]
    if start is not None:
        operands.append(start)
    if last:
        operands.append(spread)
        out_shape = jax.ShapeDtypeStruct((GROUPS, 16, 128), BF16)
    else:
        out_shape = jax.ShapeDtypeStruct((64, 512), F32)
    return pl.pallas_call(
        functools.partial(forward_kernel, targets, start is not None, last),
        in_specs=[INDEX] + [LOCAL] * len(operands),
        out_specs=LOCAL,
        out_shape=out_shape,
        compiler_params=params(),
        cost_estimate=cost(columns),
        name="forward_part",
    )(ranks, *operands)


def adjoint_kernel(targets, first, ranks, *refs):
    count = len(targets)
    field, refs = refs[0], refs[1:]
    gather = None
    if first:
        gather, refs = refs[0], refs[1:]
    right, left, refs = refs[0], refs[1], refs[2:]
    outs, refs = refs[:count], refs[count:]
    if first:
        natural = refs[0]
        received = field[...].reshape(256, 128)
        pieces = [dot_nn(gather[b], received).astype(BF16) for b in range(4)]
        for b in range(4):
            natural[:, 128 * b : 128 * b + 128] = pieces[b]
        halves = [jnp.concatenate(pieces[2 * i : 2 * i + 2], axis=1) for i in range(2)]
    else:
        halves = [field[:, 256 * i : 256 * i + 256] for i in range(2)]
    lane = lax.broadcasted_iota(jnp.int32, (64, BLOCK), 1)
    for out, (shift, slot) in zip(outs, targets):
        block = block_of(shift, slot)
        rows = rows_of(block)
        sums = None
        for i in range(2):
            products = dot_nt(halves[i], left[i, rows, :])
            coefficients = complex_pairs(products, mask_of(ranks, block, i))
            none = jnp.zeros_like(coefficients)
            spread = jnp.concatenate(
                [jnp.where(column_of(lane) == t, coefficients, none) for t in range(4)], axis=0
            )
            part = dot_nn(spread, right[i, rows, :])
            sums = part if sums is None else sums + part
        sums = sums.astype(BF16)
        for t in range(4):
            out[:, 256 * t : 256 * t + 256] = sums[64 * t : 64 * t + 64]


def adjoint_part(field, targets, ranks, right, left, gather=None):
    columns = 4 * len(targets)
    first = gather is not None
    operands = [field] + ([gather] if first else []) + [right, left]
    out_shape = [jax.ShapeDtypeStruct((64, 1024), BF16)] * len(targets)
    if first:
        out_shape.append(jax.ShapeDtypeStruct((64, 512), BF16))
    return pl.pallas_call(
        functools.partial(adjoint_kernel, targets, first),
        in_specs=[INDEX] + [LOCAL] * len(operands),
        out_specs=[LOCAL] * len(out_shape),
        out_shape=out_shape,
        compiler_params=params(),
        cost_estimate=cost(columns),
        name="adjoint_part",
    )(ranks, *operands)


def sum_kernel(first, second, third, out):
    total = first[...].astype(F32) + second[...].astype(F32) + third[...].astype(F32)
    out[...] = total.astype(BF16)


def sum_alone(*terms):
    return pl.pallas_call(
        sum_kernel,
        in_specs=[LOCAL] * 3,
        out_specs=LOCAL,
        out_shape=jax.ShapeDtypeStruct(terms[0].shape, BF16),
        compiler_params=params(),
        cost_estimate=pl.CostEstimate(flops=200_000, bytes_accessed=500_000, transcendentals=0),
        name="sum_alone",
    )(*terms)


def window_kernel(field, onset, to_time, to_freq, out):
    received = field[...].reshape(256, 128)
    signal = dot_nn(to_time[0], received) + dot_nn(to_time[1], received)
    signal = signal.reshape(8, SAMPLE_PAD, 128)
    time = lax.broadcasted_iota(jnp.int32, signal.shape, 1)
    kept = jnp.where(time < onset[...][:, None, :], signal, 0.0).reshape(8 * SAMPLE_PAD, 128)
    high = kept.astype(BF16)
    low = (kept - high.astype(F32)).astype(BF16)
    back = dot_nn(to_freq[0], high) + dot_nn(to_freq[1], high) + dot_nn(to_freq[0], low)
    out[...] = back.astype(BF16).reshape(GROUPS, 16, 128)


def window_block(field, onset, to_time, to_freq):
    return pl.pallas_call(
        window_kernel,
        out_shape=jax.ShapeDtypeStruct((GROUPS, 16, 128), BF16),
        compiler_params=pltpu.CompilerParams(vmem_limit_bytes=16 * 1024 * 1024),
        cost_estimate=pl.CostEstimate(flops=200_000_000, bytes_accessed=1_000_000, transcendentals=0),
        name="window",
    )(field, onset, to_time, to_freq)


def exchange(value):
    return lax.all_to_all(value, "freq", split_axis=0, concat_axis=0, tiled=True)


def add(*terms):
    total = terms[0].astype(F32)
    for term in terms[1:]:
        total = total + term.astype(F32)
    return total.astype(BF16)


def on_device(left_factors, right_factors, tile_ranks, window_onset, direct_wave):
    left = left_factors.reshape(2, 4096, 256)
    right = right_factors.reshape(2, 4096, 256)
    ranks = tile_ranks.reshape(2, 64)
    onset = jnp.transpose(window_onset.reshape(4, 128, 2), (0, 2, 1)).reshape(8, 128)
    to_time, to_freq, spread, gather = [jnp.asarray(table) for table in tables()]

    direct = direct_wave.reshape(64, 1024)
    direct_other = permute(direct, ACROSS)
    own, other = direct, direct_other
    minus_field = None
    current = None
    for iteration in range(ITERS):
        if iteration == 0:
            total = opening_part([own], OWN[:1], ranks, right, left)
            streams = [permute(own, UP), permute(own, DOWN)]
            other, total = lax.optimization_barrier((other, total))
            streams += [permute(other, UP), permute(other, DOWN)]
        else:
            total = forward_part([own, other], OWN, ranks, right, left)
            streams = [permute(own, UP), permute(own, DOWN), permute(other, UP), permute(other, DOWN)]
        for step in range(1, HALF):
            held = list(streams)
            streams[0], total = lax.optimization_barrier((streams[0], total))
            if step < HALF - 1:
                streams = [permute(chunk, (UP, DOWN)[n % 2]) for n, chunk in enumerate(streams)]
            else:
                streams = [permute(streams[0], UP), permute(streams[3], DOWN)]
            targets = ring_targets(step)
            if step == 1 and iteration == 0:
                held, targets = [other] + held, ((0, 1),) + targets
            total = forward_part(held, targets, ranks, right, left, start=total)
        reflected = forward_part(streams, FAR, ranks, right, left, start=total, spread=spread)
        windowed = window_block(exchange(reflected), onset, to_time, to_freq)
        received = exchange(windowed)
        far_own, far_other, minus_field = adjoint_part(received, FAR, ranks, right, left, gather=gather)
        field = minus_field
        coming = [permute(far_own, UP), None, None, permute(far_other, DOWN)]
        for step in range(HALF - 1, 0, -1):
            terms = adjoint_part(field, ring_targets(-step), ranks, right, left)
            terms = [term if came is None else add(term, came) for term, came in zip(terms, coming)]
            coming = [permute(term, (UP, DOWN)[n % 2]) for n, term in enumerate(terms)]
            field, _ = lax.optimization_barrier((field, terms[0]))
        own_term, other_term = adjoint_part(field, OWN, ranks, right, left)
        other_sum = add(other_term, coming[2], coming[3])
        own_sum = (sum_alone if iteration < ITERS - 1 else add)(own_term, coming[0], coming[1])
        own = add(direct, own_sum, permute(other_sum, ACROSS))
        if iteration < ITERS - 1:
            other = add(direct_other, other_sum, permute(own_sum, ACROSS))
        else:
            current = own
    return (current.reshape(1, 2, 32, 1024), minus_field.reshape(1, 2, 32, 512))


def solution(mesh):
    in_specs = (
        P("freq", "rows", None, None, None, None),
        P("freq", "rows", None, None, None, None),
        P("freq", "rows", None),
        P("rows", "freq"),
        P("freq", None, None, "rows"),
    )
    out_specs = (P("freq", None, None, "rows"), P("freq", None, None, "rows"))
    return jax.shard_map(
        on_device, mesh=mesh, in_specs=in_specs, out_specs=out_specs, check_vma=False
    )
```
